32 devices in a mesh: leaf: 4 (over z), row: 4 (over y, x), col: 2 (over core).
Axes of the slice: x: 2, y: 2, z: 4, core: 2. Of those that a mesh axis runs over, the one named last changes fastest.
Arguments:
- left_panels: float32 [4, 1024, 1024], P('leaf', 'row', 'col'), may hold values from -6 to 6
- upper_panels: float32 [4, 1024, 6144], P('leaf', 'row', 'col'), may hold values from -0.1875 to 0.1875
- row_blocks: int32 [4, 4], P('leaf', 'row'), may hold values from 0 to 1
- col_blocks: int32 [4, 24], P('leaf', 'col'), may hold values from 0 to 1
- ancestor: float32 [1024, 6144], P('row', 'col'), may hold values from -60 to 60
Outputs:
- equilibrated: float32 [1024, 6144], P('row', ('col', 'leaf'))
The draws below stay inside these ranges and needn't reach their ends.
All inputs are finite; a program needn't handle non-finite values. Where the reference program divides by a largest or mean magnitude, that divisor is 1e-20 or more.
Results may differ from the reference program's by a relative error of at most 0.00011.
Values sent between devices are 32-bit elements; how exact they have to be, the bound alone decides.
No kernel may reach another device: no remote copies, remote signals or barrier semaphores. Data moves between devices by JAX's collectives and lax.ppermute only.
A program may use at most 64 MiB of HBM per device.

```python
import jax
import jax.numpy as jnp
from jax import lax

M = 6144
K = 1024
BLK = 256
ROWS = 1024
MB = 24
RB = 4
SUB = 4


def block_flags(key, count):
    level = jax.random.randint(jax.random.fold_in(key, 11), (SUB, 1), 1, 5)
    values = jax.random.randint(jax.random.fold_in(key, 12), (SUB, count), 0, 4)
    return (values < level).astype(jnp.int32)


def draw_row_blocks(key, part):
    return block_flags(jax.random.fold_in(key, 1), RB)


def draw_col_blocks(key, part):
    return block_flags(jax.random.fold_in(key, 2), MB)


def draw_ancestor(key, part):
    key_z = jax.random.fold_in(key, 21)
    key_r = jax.random.fold_in(key, 22)
    key_c = jax.random.fold_in(key, 23)
    base = jnp.clip(jax.random.normal(key_z, (ROWS, M), jnp.float32), -5.0, 5.0)
    row_scale = jnp.exp(jax.random.uniform(key_r, (ROWS, 1), jnp.float32, 0.0, 1.15))
    col_scale = jnp.exp(jax.random.uniform(key_c, (1, M), jnp.float32, 0.0, 1.15))
    return base * row_scale * col_scale


def steps_of(own_key, shape, cuts, low, high):
    def one(axis_at, blocks):
        heights = jax.random.uniform(jax.random.fold_in(jax.random.fold_in(own_key, 6), axis_at), (blocks,), jnp.float32, low / len(cuts), high / len(cuts))
        return jnp.repeat(jnp.exp(heights), shape[axis_at] // blocks).reshape((-1,) + (1,) * (len(shape) - axis_at - 1))

    level = one(*cuts[0])
    for cut in cuts[1:]:
        level = level * one(*cut)
    return level


def noise(rng, shape, width, limit, split=(), kind=jnp.bfloat16):
    entries = width * jax.random.normal(rng, shape, jnp.float32)
    if split:
        entries = entries * steps_of(rng, shape, split, -0.22, 0.18)
    return jnp.clip(entries, -limit, limit).astype(kind)


def setup_inputs(seed: int = 0) -> dict:
    streams_of = jax.random.split(jax.random.key(seed), 6)
    return {
        "left_panels": noise(streams_of[0], (SUB, ROWS, K), 1.0, 6.0, ((0, 4), (1, 4), (2, 2)), jnp.float32),
        "upper_panels": noise(streams_of[1], (SUB, K, M), K ** -0.5, 0.1875, ((0, 4), (1, 4), (2, 2)), jnp.float32),
        "row_blocks": draw_row_blocks(jax.random.fold_in(streams_of[5], 71), 0),
        "col_blocks": draw_col_blocks(jax.random.fold_in(streams_of[5], 71), 0),
        "ancestor": draw_ancestor(jax.random.fold_in(streams_of[5], 71), 0),
    }


def reference(left_panels, upper_panels, row_blocks, col_blocks, ancestor):
    row_mask = jnp.repeat((row_blocks > 0).astype(jnp.float32), BLK, axis=1)
    col_mask = jnp.repeat((col_blocks > 0).astype(jnp.float32), BLK, axis=1)
    schur = jnp.zeros((ROWS, M), jnp.float32)
    for subtree in range(SUB):
        lower = left_panels[subtree] * row_mask[subtree][:, None]
        upper = upper_panels[subtree] * col_mask[subtree][None, :]
        schur = schur + jnp.dot(lower, upper, precision=lax.Precision.HIGHEST, preferred_element_type=jnp.float32)
    updated = ancestor - schur
    peak = jnp.max(jnp.abs(updated), axis=1)
    return updated / (peak[:, None] + 1e-6)
```

```python
import jax
import jax.numpy as jnp
from jax import lax
from jax.sharding import PartitionSpec as P

LANES = 128
HIGHEST = lax.Precision.HIGHEST


def swap(value, axis, size, bit):
    return lax.ppermute(value, axis, [(i, i ^ bit) for i in range(size)])


def butterfly_max(value, axis):
    size = lax.axis_size(axis)
    if size & (size - 1):
        return lax.pmax(value, axis)
    bit = 1
    while bit < size:
        value = jnp.maximum(value, swap(value, axis, size, bit))
        bit *= 2
    return value


def bit_order(count):
    order = [0]
    bit = 1
    while bit < count:
        order = order + [i + bit for i in order]
        bit *= 2
    width = count.bit_length() - 1
    return [int(format(i, "b").zfill(width)[::-1], 2) if width else 0 for i in range(count)]


def dot(a, b):
    return jnp.dot(a, b, precision=HIGHEST, preferred_element_type=jnp.float32)


def plain(left, upper, row_on, col_on, ancestor):
    lower = left * row_on
    upper_full = lax.all_gather(upper, "row", axis=0, tiled=True)
    lower_full = lax.all_gather(lower, "col", axis=1, tiled=True)
    partial_value = dot(lower_full, upper_full) * col_on[None, :]
    leaf_count = lax.axis_size("leaf")
    share_cols = upper.shape[1] // leaf_count
    schur = lax.psum_scatter(partial_value, "leaf", scatter_dimension=1, tiled=True)
    share = lax.dynamic_slice_in_dim(ancestor, lax.axis_index("leaf") * share_cols, share_cols, 1)
    updated = share - schur
    peak = lax.pmax(jnp.max(jnp.abs(updated), axis=1), ("leaf", "col"))
    return updated / (peak[:, None] + 1e-6)


def chunked(left, upper, row_on, col_on, ancestor):
    leaf_count, rows, cols = (lax.axis_size(a) for a in ("leaf", "row", "col"))
    leaf, row, col = (lax.axis_index(a) for a in ("leaf", "row", "col"))
    low_one, high_one = row % 2 == 1, row // 2 == 1
    depth = upper.shape[0]
    share_cols = upper.shape[1] // leaf_count
    order = bit_order(leaf_count)

    lower = left * row_on
    first, second = lower[:, :depth], lower[:, depth:]
    mine = jnp.where(low_one, second, first)
    theirs = swap(jnp.where(low_one, first, second), "row", rows, 1)
    here = jnp.concatenate([theirs, mine], 0)
    there = swap(here, "col", cols, 1)
    aligned = (col == 1) == high_one
    left_own = jnp.where(aligned, here, there)
    left_other = jnp.where(aligned, there, here)

    step = LANES
    pieces = []
    for at in range(0, share_cols, step):
        spans = [(s * share_cols + at, s * share_cols + min(at + step, share_cols)) for s in order]
        block = jnp.concatenate([upper[:, a:b] for a, b in spans], 1)
        on = jnp.concatenate([col_on[a:b] for a, b in spans], 0)[None, :]
        got = swap(block, "row", rows, 2)
        part = (dot(left_own, block) + dot(left_other, got)) * on
        half = part.shape[0] // 2
        total = part[half:] + swap(part[:half], "row", rows, 1)
        bit = 1
        while bit < leaf_count:
            half = total.shape[1] // 2
            upper_half = (leaf // bit) % 2 == 1
            send = jnp.where(upper_half, total[:, :half], total[:, half:])
            keep = jnp.where(upper_half, total[:, half:], total[:, :half])
            total = keep + swap(send, "leaf", leaf_count, bit)
            bit *= 2
        pieces.append(total)
    schur = jnp.concatenate(pieces, 1)
    share = lax.dynamic_slice_in_dim(ancestor, leaf * share_cols, share_cols, 1)
    updated = share - schur
    peak = butterfly_max(butterfly_max(jnp.max(jnp.abs(updated), axis=1), "col"), "leaf")
    return updated / (peak[:, None] + 1e-6)


def solution(mesh):
    leaf_count, rows, cols = (mesh.shape[a] for a in ("leaf", "row", "col"))
    fits = rows == 4 and cols == 2 and leaf_count & (leaf_count - 1) == 0

    def shards(left_panels, upper_panels, row_blocks, col_blocks, ancestor):
        row_each = left_panels.shape[1] // row_blocks.shape[1]
        col_each = upper_panels.shape[2] // col_blocks.shape[1]
        row_on = jnp.repeat((row_blocks[0] > 0).astype(jnp.float32), row_each)[:, None]
        col_on = jnp.repeat((col_blocks[0] > 0).astype(jnp.float32), col_each)
        body = chunked if fits else plain
        return body(left_panels[0], upper_panels[0], row_on, col_on, ancestor)

    return jax.shard_map(
        shards,
        mesh=mesh,
        in_specs=(
            P("leaf", "row", "col"),
            P("leaf", "row", "col"),
            P("leaf", "row"),
            P("leaf", "col"),
            P("row", "col"),
        ),
        out_specs=P("row", ("col", "leaf")),
        check_vma=False,
    )
```

```python
import functools

import jax
import jax.numpy as jnp
from jax import lax
from jax.experimental import pallas as pl
from jax.experimental.pallas import tpu as pltpu
from jax.sharding import PartitionSpec as P

LANES = 128
F32, BF16 = jnp.float32, jnp.bfloat16
VMEM = "whole"
SMEM = pl.BlockSpec(memory_space=pltpu.SMEM)
ANY = pl.BlockSpec(memory_space=pl.ANY)

PANEL_ROUNDS = (
    ("n00n", ((1, 0), (2, 0), (2, 1), (1, 1))),
    ("011x", (None, (2, 0), (2, 1), (0, 1))),
    ("0nn0", ((0, 1), (1, 1), (1, 0), None)),
    ("1x00", ((0, 1), (0, 1), None, None)),
)
SHARES = (0, 2, 1, 3)
PORTIONS = (2, 2, 2, 2, 2, 2)


def dot(a, b):
    return jnp.dot(a, b, precision=lax.Precision.HIGHEST, preferred_element_type=F32)


def plain(left, upper, row_blocks, col_blocks, ancestor):
    row_on = jnp.repeat((row_blocks[0] > 0).astype(F32), left.shape[0] // row_blocks.shape[1])[:, None]
    col_on = jnp.repeat((col_blocks[0] > 0).astype(F32), upper.shape[1] // col_blocks.shape[1])[None, :]
    upper_full = lax.all_gather(upper, "row", axis=0, tiled=True)
    lower_full = lax.all_gather(left * row_on, "col", axis=1, tiled=True)
    leaf_count = lax.axis_size("leaf")
    share_cols = upper.shape[1] // leaf_count
    schur = lax.psum_scatter(dot(lower_full, upper_full) * col_on, "leaf", scatter_dimension=1, tiled=True)
    share = lax.dynamic_slice_in_dim(ancestor, lax.axis_index("leaf") * share_cols, share_cols, 1)
    updated = share - schur
    peak = lax.pmax(jnp.max(jnp.abs(updated), axis=1), ("leaf", "col"))
    return updated / (peak[:, None] + 1e-6)


def run(body, ins, outs, flops=0, limit=24):
    size = sum(4 * a.size for s, a in ins if s is VMEM) + sum(4 * o.size for o in outs)

    def whole(a):
        return pl.BlockSpec(a.shape, lambda step: (0,) * len(a.shape))

    return pl.pallas_call(
        body,
        grid=(1,),
        in_specs=[whole(a) if s is VMEM else s for s, a in ins],
        out_specs=[whole(o) for o in outs],
        out_shape=outs,
        compiler_params=pltpu.CompilerParams(vmem_limit_bytes=limit * 2**20),
        cost_estimate=pl.CostEstimate(flops=flops, bytes_accessed=size, transcendentals=0),
    )(*[a for _, a in ins])


def shape(*dims, dtype=F32):
    return jax.ShapeDtypeStruct(dims, dtype)


def split(x):
    high = x.astype(BF16)
    return high, (x - high.astype(F32)).astype(BF16)


def product(ah, al, b):
    bh, bl = split(b)
    d = functools.partial(jnp.dot, preferred_element_type=F32)
    return d(ah, bh) + (d(ah, bl) + d(al, bh))


def coordinates():
    row = lax.axis_index("row")
    return row % 2 == 1, row // 2 == 1, lax.axis_index("col") == 1


def pick(y, c, a, b, cc, d):
    return jnp.where(c, jnp.where(y, d, b), jnp.where(y, cc, a))


def copy_chunk(tiles, out, chunk):
    at, wide = chunk
    each = len(tiles) // len(SHARES)
    for k in range(len(SHARES)):
        done = 0
        for m in range(each):
            skip = (at + done) % LANES
            take = min(LANES - skip, wide - done)
            out[:, pl.ds(k * wide + done, take)] = tiles[k * each + m][:, pl.ds(skip, take)]
            done += take


def copy_message(tiles, out, chunks):
    at = 0
    for chunk in chunks:
        count = len(SHARES) * spanned(chunk)
        copy_chunk(tiles[:count], out.at[:, pl.ds(at, len(SHARES) * chunk[1])], chunk)
        tiles, at = tiles[count:], at + len(SHARES) * chunk[1]


def message_body(chunks, token, *refs):
    copy_message(refs[:-1], refs[-1], chunks)


def first_body(chunks, row_blocks, left, *refs):
    x, y, c = coordinates()
    depth = left.shape[1] // 2
    mask = jnp.where(row_blocks[0, 0] > 0, 1.0, 0.0).astype(F32)
    l0, l1 = left[:, :depth] * mask, left[:, depth:] * mask
    named = {"0": l0, "1": l1, "x": jnp.where(x, l1, l0), "n": jnp.where(x, l0, l1)}
    count = sum(len(SHARES) * spanned(c0) for c0 in chunks)
    tiles, outs = refs[:count], refs[count:]
    for out, (index, _) in zip(outs, PANEL_ROUNDS):
        out[...] = pick(y, c, *(named[k] for k in index))
    outs[4][:, :depth] = l0
    outs[4][:, depth:] = l1
    copy_message(tiles, outs[5], chunks)


def spanned(chunk):
    at, wide = chunk
    return (at + wide - 1) // LANES - at // LANES + 1


def panel_body(left, *refs):
    x, y, c = coordinates()
    height, depth = left.shape[0], left.shape[1] // 2
    r1, r2, r3, r4 = (r[...] for r in refs[:4])
    l0, l1 = left[:, :depth], left[:, depth:]
    lx = jnp.where(x, l1, l0)
    partner = pick(y, c, r1, r1, r3, r1), pick(y, c, r3, r2, r1, r2)
    own = pick(y, c, lx, r3, lx, l0), pick(y, c, r4, r4, r2, l1)
    second = jnp.logical_or(jnp.logical_and(c, x), jnp.logical_and(jnp.logical_not(c), y))
    for at in (0, 1):
        high, low = refs[4 + 2 * at:6 + 2 * at]
        for rows, pair in ((pl.ds(0, height), partner), (pl.ds(height, height), own)):
            a, b = pair[::-1] if at else pair
            high[rows], low[rows] = split(jnp.where(second, b, a))


def multiply_body(half, plan, col_blocks, ah, al, bh, bl, block, got, token, *refs):
    ranges, begin, wide, later = plan
    tiles, (send, keep), rest = refs[:-2 - bool(later)], refs[len(refs) - 2 - bool(later):][:2], refs[-1]
    own, other = block[:, pl.ds(begin, wide)], got[:, pl.ds(begin, wide)]
    for out, rows in ((send, pl.ds(0, half)), (keep, pl.ds(half, half))):
        value = product(ah[rows], al[rows], own) + product(bh[rows], bl[rows], other)
        for at, width, b in ranges:
            on = jnp.where(col_blocks[0, b] > 0, 1.0, 0.0).astype(F32)
            out[:, pl.ds(at, width)] = value[:, at:at + width] * on
    if later:
        copy_message(tiles, rest, later)


def reduce_body(jobs, *refs):
    n_in = sum(count for _, count, _ in jobs)
    ins, outs = list(refs[:n_in]), list(refs[n_in + 1:])
    leaf = lax.axis_index("leaf")
    for step, count, wide in jobs:
        mine, ins = ins[:count], ins[count:]
        send, keep, outs = outs[0], outs[1], outs[2:]
        if step == "f":
            got, kept, share, peak = mine
            value = share[...] - (kept[...] + got[...])
            send[...] = value
            top = jnp.max(jnp.abs(value), axis=1, keepdims=True)
            keep[...] = jnp.maximum(peak[...], jnp.broadcast_to(top, keep.shape))
            continue
        bit = (leaf % 2 if step == "o" else leaf // 2) == 1
        half = 2 * wide if step == "o" else wide
        total = mine[0][...] + mine[1][...]
        a, b = total[:, :half], total[:, half:]
        send[...] = jnp.where(bit, a, b)
        keep[...] = jnp.where(bit, b, a)


def swap(value, axis, size, bit):
    return lax.ppermute(value, axis, [(i, i ^ bit) for i in range(size)])


def after(value, *others):
    return lax.optimization_barrier((value,) + others)[0]


STEPS = (
    "A0", "A1", "o0", "A2", "o1t0", "A3", "o2t1", "A4", "f0o3t2", "A5", "f1o4", "t3", "f2o5", "t4", "f3t5", "f4", "f5",
)
GATHERS = ((0,), (1,), (2,), (3,), (4,), (5,))
TIES = (None, None, 0, 1, 2, 3)
FIRST = 56


def chunked(left, upper, row_blocks, col_blocks, ancestor):
    rows, cols = lax.axis_size("row"), lax.axis_size("col")
    leaf_count = lax.axis_size("leaf")
    leaf, row, col = (lax.axis_index(a).astype(jnp.int32) for a in ("leaf", "row", "col"))
    depth, height = upper.shape[0], left.shape[0]
    share_cols = upper.shape[1] // leaf_count
    block_cols = upper.shape[1] // col_blocks.shape[1]
    unit = share_cols // sum(PORTIONS)
    chunks, at = [], 0
    for p in PORTIONS:
        chunks.append((at, p * unit))
        at += p * unit
    n = len(chunks)
    def move(value, flip):
        pairs = []
        for r in range(rows):
            for c in range(cols):
                hop = flip(r, c)
                if hop is not None:
                    pairs.append((cols * r + c, cols * (r ^ hop[0]) + (c ^ hop[1])))
        return lax.ppermute(value, ("row", "col"), pairs)

    def gather(value):
        return move(value, lambda r, c: (1 if c else 2, 0))

    def exchange(value):
        return move(value, lambda r, c: (2 if c else 1, 0))

    def tiles(chunk):
        at, _ = chunk
        return [
            (pl.BlockSpec((depth, LANES), functools.partial(lambda k, step: (0, k), (s * share_cols + at) // LANES + m)), upper)
            for s in SHARES for m in range(spanned(chunk))
        ]

    def tiles_of(members):
        return [spec for i in members for spec in tiles(chunks[i])]

    def widths(members):
        return 4 * sum(chunks[i][1] for i in members)

    first = run(
        functools.partial(first_body, [chunks[i] for i in GATHERS[0]]),
        [(SMEM, row_blocks), (VMEM, left)] + tiles_of(GATHERS[0]),
        [shape(height, depth)] * 4 + [shape(height, 2 * depth), shape(depth, widths(GATHERS[0]))],
        limit=FIRST,
    )
    blocks, gots = {0: first[5]}, {0: gather(first[5])}
    landed = [move(v, lambda r, c, hops=hops: hops[(r // 2) * 2 + c]) for v, (_, hops) in zip(first[:4], PANEL_ROUNDS)]
    lower = first[4]
    for g, tie in enumerate(TIES):
        if g and tie is None:
            blocks[g], = run(
                functools.partial(message_body, [chunks[i] for i in GATHERS[g]]),
                [(ANY, lower)] + tiles_of(GATHERS[g]), [shape(depth, widths(GATHERS[g]))], limit=FIRST,
            )
            gots[g] = gather(blocks[g])
    halves = run(panel_body, [(VMEM, lower)] + [(VMEM, v) for v in landed], [shape(2 * height, depth, dtype=BF16)] * 4)

    share = lax.dynamic_slice_in_dim(after(ancestor, halves[0]), leaf * share_cols, share_cols, 1)
    x_got, kept, z1, z1_kept, z2, z2_kept, upds = ({} for _ in range(7))
    peak = jnp.zeros((height, LANES), F32)
    token = lower
    for word in STEPS:
        if word[0] == "A":
            t = int(word[1:])
            at, wide = chunks[t]
            ranges = []
            for k, s in enumerate(SHARES):
                start = s * share_cols + at
                end, base = start + wide, start
                while start < end:
                    stop = min(end, (start // block_cols + 1) * block_cols)
                    ranges.append((k * wide + start - base, stop - start, start // block_cols))
                    start = stop
            g = [t in members for members in GATHERS].index(True)
            begin = widths([i for i in GATHERS[g] if i < t])
            later = [k for k, tie in enumerate(TIES) if tie == t]
            members = [chunks[i] for k in later for i in GATHERS[k]]
            res = run(
                functools.partial(multiply_body, height, (ranges, begin, 4 * wide, members)),
                [(SMEM, col_blocks)] + [(VMEM, h) for h in halves] + [(VMEM, blocks[g]), (VMEM, gots[g]), (ANY, token)]
                + [spec for k in later for spec in tiles_of(GATHERS[k])],
                [shape(height, 4 * wide)] * 2 + [shape(depth, widths(GATHERS[k])) for k in later],
                flops=48 * height * depth * wide,
            )
            kept[t] = token = res[1]
            for k in later:
                blocks[k] = res[2]
                gots[k] = gather(res[2])
            x_got[t] = exchange(res[0])
            continue
        todo = [(word[i], int(word[i + 1])) for i in range(0, len(word), 2)]
        jobs, ins, outs = [], [], []
        for step, t in todo:
            at, wide = chunks[t]
            if step == "o":
                mine, new = [x_got[t], kept[t]], [shape(height, 2 * wide)] * 2
            elif step == "t":
                mine, new = [z1[t], z1_kept[t]], [shape(height, wide)] * 2
            else:
                mine, new = [z2[t], z2_kept[t], share[:, at:at + wide], peak], [shape(height, wide), shape(height, LANES)]
            jobs.append((step, len(mine), wide))
            ins += [(VMEM, v) for v in mine]
            outs += new
        res = run(functools.partial(reduce_body, jobs), ins + [(ANY, token)], outs)
        token = res[1]
        tops = []
        for k, (step, t) in enumerate(todo):
            a, b = res[2 * k], res[2 * k + 1]
            if step == "o":
                z1[t], z1_kept[t] = swap(a, "leaf", leaf_count, 1), b
            elif step == "t":
                z2[t], z2_kept[t] = swap(a, "leaf", leaf_count, 2), b
            else:
                upds[t] = a
                tops.append(b)
        if tops:
            peak = functools.reduce(jnp.maximum, tops)

    updated = jnp.concatenate([upds[g] for g in range(n)], 1)
    top = jnp.max(peak, axis=1)
    top = jnp.maximum(top, swap(top, "col", cols, 1))
    for bit in (1, 2):
        top = jnp.maximum(top, swap(top, "leaf", leaf_count, bit))
    return updated / (top[:, None] + 1e-6)


def solution(mesh):
    leaf_count, rows, cols = (mesh.shape[a] for a in ("leaf", "row", "col"))

    def shards(left_panels, upper_panels, row_blocks, col_blocks, ancestor):
        share_cols = upper_panels.shape[2] // leaf_count
        fits = (
            rows == 4 and cols == 2 and leaf_count == 4
            and share_cols % (sum(PORTIONS) * 64) == 0
            and left_panels.shape[2] == 2 * upper_panels.shape[1]
            and row_blocks.shape[1] == 1
        )
        body = chunked if fits else plain
        return body(left_panels[0], upper_panels[0], row_blocks, col_blocks, ancestor)

    return jax.shard_map(
        shards,
        mesh=mesh,
        in_specs=(
            P("leaf", "row", "col"),
            P("leaf", "row", "col"),
            P("leaf", "row"),
            P("leaf", "col"),
            P("row", "col"),
        ),
        out_specs=P("row", ("col", "leaf")),
        check_vma=False,
    )
```

```python
import functools

import jax
import jax.numpy as jnp
from jax import lax
from jax.experimental import pallas as pl
from jax.experimental.pallas import tpu as pltpu
from jax.sharding import PartitionSpec as P

LANES = 128
F32, BF16 = jnp.float32, jnp.bfloat16
VMEM = "whole"
SMEM = pl.BlockSpec(memory_space=pltpu.SMEM)
ANY = pl.BlockSpec(memory_space=pl.ANY)

PANEL_ROUNDS = (
    ("n00n", ((1, 0), (2, 0), (2, 1), (1, 1))),
    ("011x", (None, (2, 0), (2, 1), (0, 1))),
    ("0nn0", ((0, 1), (1, 1), (1, 0), None)),
    ("1x00", ((0, 1), (0, 1), None, None)),
)
SHARES = (0, 2, 1, 3)
PORTIONS = (2, 2, 2, 2, 2, 2)


def dot(a, b):
    return jnp.dot(a, b, precision=lax.Precision.HIGHEST, preferred_element_type=F32)


def plain(left, upper, row_blocks, col_blocks, ancestor):
    row_on = jnp.repeat((row_blocks[0] > 0).astype(F32), left.shape[0] // row_blocks.shape[1])[:, None]
    col_on = jnp.repeat((col_blocks[0] > 0).astype(F32), upper.shape[1] // col_blocks.shape[1])[None, :]
    upper_full = lax.all_gather(upper, "row", axis=0, tiled=True)
    lower_full = lax.all_gather(left * row_on, "col", axis=1, tiled=True)
    leaf_count = lax.axis_size("leaf")
    share_cols = upper.shape[1] // leaf_count
    schur = lax.psum_scatter(dot(lower_full, upper_full) * col_on, "leaf", scatter_dimension=1, tiled=True)
    share = lax.dynamic_slice_in_dim(ancestor, lax.axis_index("leaf") * share_cols, share_cols, 1)
    updated = share - schur
    peak = lax.pmax(jnp.max(jnp.abs(updated), axis=1), ("leaf", "col"))
    return updated / (peak[:, None] + 1e-6)


def run(body, ins, outs, flops=0, limit=24):
    size = sum(4 * a.size for s, a in ins if s is VMEM) + sum(4 * o.size for o in outs)

    def whole(a):
        return pl.BlockSpec(a.shape, lambda step: (0,) * len(a.shape))

    return pl.pallas_call(
        body,
        grid=(1,),
        in_specs=[whole(a) if s is VMEM else s for s, a in ins],
        out_specs=[whole(o) for o in outs],
        out_shape=outs,
        compiler_params=pltpu.CompilerParams(vmem_limit_bytes=limit * 2**20),
        cost_estimate=pl.CostEstimate(flops=flops, bytes_accessed=size, transcendentals=0),
    )(*[a for _, a in ins])


def shape(*dims, dtype=F32):
    return jax.ShapeDtypeStruct(dims, dtype)


def split(x):
    high = x.astype(BF16)
    return high, (x - high.astype(F32)).astype(BF16)


def product(ah, al, b):
    bh, bl = split(b)
    d = functools.partial(jnp.dot, preferred_element_type=F32)
    return d(ah, bh) + (d(ah, bl) + d(al, bh))


def coordinates():
    row = lax.axis_index("row")
    return row % 2 == 1, row // 2 == 1, lax.axis_index("col") == 1


def pick(y, c, a, b, cc, d):
    return jnp.where(c, jnp.where(y, d, b), jnp.where(y, cc, a))


def copy_chunk(tiles, out, chunk):
    at, wide = chunk
    each = len(tiles) // len(SHARES)
    for k in range(len(SHARES)):
        done = 0
        for m in range(each):
            skip = (at + done) % LANES
            take = min(LANES - skip, wide - done)
            out[:, pl.ds(k * wide + done, take)] = tiles[k * each + m][:, pl.ds(skip, take)]
            done += take


def copy_message(tiles, out, chunks):
    at = 0
    for chunk in chunks:
        count = len(SHARES) * spanned(chunk)
        copy_chunk(tiles[:count], out.at[:, pl.ds(at, len(SHARES) * chunk[1])], chunk)
        tiles, at = tiles[count:], at + len(SHARES) * chunk[1]


def message_body(chunks, token, *refs):
    copy_message(refs[:-1], refs[-1], chunks)


def first_body(chunks, row_blocks, left, *refs):
    x, y, c = coordinates()
    depth = left.shape[1] // 2
    mask = jnp.where(row_blocks[0, 0] > 0, 1.0, 0.0).astype(F32)
    l0, l1 = left[:, :depth] * mask, left[:, depth:] * mask
    named = {"0": l0, "1": l1, "x": jnp.where(x, l1, l0), "n": jnp.where(x, l0, l1)}
    count = sum(len(SHARES) * spanned(c0) for c0 in chunks)
    tiles, outs = refs[:count], refs[count:]
    for out, (index, _) in zip(outs, PANEL_ROUNDS):
        out[...] = pick(y, c, *(named[k] for k in index))
    outs[4][:, :depth] = l0
    outs[4][:, depth:] = l1
    copy_message(tiles, outs[5], chunks)


def spanned(chunk):
    at, wide = chunk
    return (at + wide - 1) // LANES - at // LANES + 1


def panel_body(left, *refs):
    x, y, c = coordinates()
    height, depth = left.shape[0], left.shape[1] // 2
    r1, r2, r3, r4 = (r[...] for r in refs[:4])
    l0, l1 = left[:, :depth], left[:, depth:]
    lx = jnp.where(x, l1, l0)
    partner = pick(y, c, r1, r1, r3, r1), pick(y, c, r3, r2, r1, r2)
    own = pick(y, c, lx, r3, lx, l0), pick(y, c, r4, r4, r2, l1)
    second = jnp.logical_or(jnp.logical_and(c, x), jnp.logical_and(jnp.logical_not(c), y))
    for at in (0, 1):
        high, low = refs[4 + 2 * at:6 + 2 * at]
        for rows, pair in ((pl.ds(0, height), partner), (pl.ds(height, height), own)):
            a, b = pair[::-1] if at else pair
            high[rows], low[rows] = split(jnp.where(second, b, a))


def multiply_body(half, plan, col_blocks, ah, al, bh, bl, block, got, token, *refs):
    ranges, begin, wide, later = plan
    tiles, (send, keep), rest = refs[:-2 - bool(later)], refs[len(refs) - 2 - bool(later):][:2], refs[-1]
    own, other = block[:, pl.ds(begin, wide)], got[:, pl.ds(begin, wide)]
    for out, rows in ((send, pl.ds(0, half)), (keep, pl.ds(half, half))):
        value = product(ah[rows], al[rows], own) + product(bh[rows], bl[rows], other)
        for at, width, b in ranges:
            on = jnp.where(col_blocks[0, b] > 0, 1.0, 0.0).astype(F32)
            out[:, pl.ds(at, width)] = value[:, at:at + width] * on
    if later:
        copy_message(tiles, rest, later)


def reduce_body(jobs, *refs):
    n_in = sum(count for _, count, _ in jobs)
    ins, outs = list(refs[:n_in]), list(refs[n_in + 1:])
    leaf = lax.axis_index("leaf")
    for step, count, wide in jobs:
        mine, ins = ins[:count], ins[count:]
        send, keep, outs = outs[0], outs[1], outs[2:]
        if step == "f":
            got, kept, share, peak = mine
            value = share[...] - (kept[...] + got[...])
            send[...] = value
            top = jnp.max(jnp.abs(value), axis=1, keepdims=True)
            keep[...] = jnp.maximum(peak[...], jnp.broadcast_to(top, keep.shape))
            continue
        bit = (leaf % 2 if step == "o" else leaf // 2) == 1
        half = 2 * wide if step == "o" else wide
        total = mine[0][...] + mine[1][...]
        a, b = total[:, :half], total[:, half:]
        send[...] = jnp.where(bit, a, b)
        keep[...] = jnp.where(bit, b, a)


def swap(value, axis, size, bit):
    return lax.ppermute(value, axis, [(i, i ^ bit) for i in range(size)])


def after(value, *others):
    return lax.optimization_barrier((value,) + others)[0]


STEPS = (
    "A0", "A1", "o0", "o1t0", "A2", "A3", "o2t1", "A4", "f0", "o3t2", "A5", "f1o4", "f2o5", "t3", "t4", "f3t5", "f5",
    "f4",
)
GATHERS = ((0,), (1,), (2,), (3,), (4,), (5,))
TIES = (None, None, 0, 1, 2, 3)
FIRST = 56


def chunked(left, upper, row_blocks, col_blocks, ancestor):
    rows, cols = lax.axis_size("row"), lax.axis_size("col")
    leaf_count = lax.axis_size("leaf")
    leaf, row, col = (lax.axis_index(a).astype(jnp.int32) for a in ("leaf", "row", "col"))
    depth, height = upper.shape[0], left.shape[0]
    share_cols = upper.shape[1] // leaf_count
    block_cols = upper.shape[1] // col_blocks.shape[1]
    unit = share_cols // sum(PORTIONS)
    chunks, at = [], 0
    for p in PORTIONS:
        chunks.append((at, p * unit))
        at += p * unit
    n = len(chunks)
    def move(value, flip):
        pairs = []
        for r in range(rows):
            for c in range(cols):
                hop = flip(r, c)
                if hop is not None:
                    pairs.append((cols * r + c, cols * (r ^ hop[0]) + (c ^ hop[1])))
        return lax.ppermute(value, ("row", "col"), pairs)

    def gather(value):
        return move(value, lambda r, c: (1 if c else 2, 0))

    def exchange(value):
        return move(value, lambda r, c: (2 if c else 1, 0))

    def tiles(chunk):
        at, _ = chunk
        return [
            (pl.BlockSpec((depth, LANES), functools.partial(lambda k, step: (0, k), (s * share_cols + at) // LANES + m)), upper)
            for s in SHARES for m in range(spanned(chunk))
        ]

    def tiles_of(members):
        return [spec for i in members for spec in tiles(chunks[i])]

    def widths(members):
        return 4 * sum(chunks[i][1] for i in members)

    first = run(
        functools.partial(first_body, [chunks[i] for i in GATHERS[0]]),
        [(SMEM, row_blocks), (VMEM, left)] + tiles_of(GATHERS[0]),
        [shape(height, depth)] * 4 + [shape(height, 2 * depth), shape(depth, widths(GATHERS[0]))],
        limit=FIRST,
    )
    blocks, gots = {0: first[5]}, {0: gather(first[5])}
    landed = [move(v, lambda r, c, hops=hops: hops[(r // 2) * 2 + c]) for v, (_, hops) in zip(first[:4], PANEL_ROUNDS)]
    lower = first[4]
    for g, tie in enumerate(TIES):
        if g and tie is None:
            blocks[g], = run(
                functools.partial(message_body, [chunks[i] for i in GATHERS[g]]),
                [(ANY, lower)] + tiles_of(GATHERS[g]), [shape(depth, widths(GATHERS[g]))], limit=FIRST,
            )
            gots[g] = gather(blocks[g])
    halves = run(panel_body, [(VMEM, lower)] + [(VMEM, v) for v in landed], [shape(2 * height, depth, dtype=BF16)] * 4)

    share = lax.dynamic_slice_in_dim(after(ancestor, halves[0]), leaf * share_cols, share_cols, 1)
    x_got, kept, z1, z1_kept, z2, z2_kept, upds = ({} for _ in range(7))
    peak = jnp.zeros((height, LANES), F32)
    token = a_token = lower
    for word in STEPS:
        if word[0] == "A":
            t = int(word[1:])
            at, wide = chunks[t]
            ranges = []
            for k, s in enumerate(SHARES):
                start = s * share_cols + at
                end, base = start + wide, start
                while start < end:
                    stop = min(end, (start // block_cols + 1) * block_cols)
                    ranges.append((k * wide + start - base, stop - start, start // block_cols))
                    start = stop
            g = [t in members for members in GATHERS].index(True)
            begin = widths([i for i in GATHERS[g] if i < t])
            later = [k for k, tie in enumerate(TIES) if tie == t]
            members = [chunks[i] for k in later for i in GATHERS[k]]
            res = run(
                functools.partial(multiply_body, height, (ranges, begin, 4 * wide, members)),
                [(SMEM, col_blocks)] + [(VMEM, h) for h in halves] + [(VMEM, blocks[g]), (VMEM, gots[g]), (ANY, a_token)]
                + [spec for k in later for spec in tiles_of(GATHERS[k])],
                [shape(height, 4 * wide)] * 2 + [shape(depth, widths(GATHERS[k])) for k in later],
                flops=48 * height * depth * wide,
            )
            kept[t] = a_token = res[1]
            token = res[1]
            for k in later:
                blocks[k] = res[2]
                gots[k] = gather(res[2])
            x_got[t] = exchange(res[0])
            continue
        todo = [(word[i], int(word[i + 1])) for i in range(0, len(word), 2)]
        jobs, ins, outs = [], [], []
        for step, t in todo:
            at, wide = chunks[t]
            if step == "o":
                mine, new = [x_got[t], kept[t]], [shape(height, 2 * wide)] * 2
            elif step == "t":
                mine, new = [z1[t], z1_kept[t]], [shape(height, wide)] * 2
            else:
                mine, new = [z2[t], z2_kept[t], share[:, at:at + wide], peak], [shape(height, wide), shape(height, LANES)]
            jobs.append((step, len(mine), wide))
            ins += [(VMEM, v) for v in mine]
            outs += new
        res = run(functools.partial(reduce_body, jobs), ins + [(ANY, token)], outs)
        token = res[1]
        a_token = res[1]
        tops = []
        for k, (step, t) in enumerate(todo):
            a, b = res[2 * k], res[2 * k + 1]
            if step == "o":
                z1[t], z1_kept[t] = swap(a, "leaf", leaf_count, 1), b
            elif step == "t":
                z2[t], z2_kept[t] = swap(a, "leaf", leaf_count, 2), b
            else:
                upds[t] = a
                tops.append(b)
        if tops:
            peak = functools.reduce(jnp.maximum, tops)

    updated = jnp.concatenate([upds[g] for g in range(n)], 1)
    top = jnp.max(peak, axis=1)
    top = jnp.maximum(top, swap(top, "col", cols, 1))
    for bit in (1, 2):
        top = jnp.maximum(top, swap(top, "leaf", leaf_count, bit))
    return updated / (top[:, None] + 1e-6)


def solution(mesh):
    leaf_count, rows, cols = (mesh.shape[a] for a in ("leaf", "row", "col"))

    def shards(left_panels, upper_panels, row_blocks, col_blocks, ancestor):
        share_cols = upper_panels.shape[2] // leaf_count
        fits = (
            rows == 4 and cols == 2 and leaf_count == 4
            and share_cols % (sum(PORTIONS) * 64) == 0
            and left_panels.shape[2] == 2 * upper_panels.shape[1]
            and row_blocks.shape[1] == 1
        )
        body = chunked if fits else plain
        return body(left_panels[0], upper_panels[0], row_blocks, col_blocks, ancestor)

    return jax.shard_map(
        shards,
        mesh=mesh,
        in_specs=(
            P("leaf", "row", "col"),
            P("leaf", "row", "col"),
            P("leaf", "row"),
            P("leaf", "col"),
            P("row", "col"),
        ),
        out_specs=P("row", ("col", "leaf")),
        check_vma=False,
    )
```

```python
import functools

import jax
import jax.numpy as jnp
from jax import lax
from jax.experimental import pallas as pl
from jax.experimental.pallas import tpu as pltpu
from jax.sharding import PartitionSpec as P

LANES = 128
F32, BF16 = jnp.float32, jnp.bfloat16
VMEM = "whole"
SMEM = pl.BlockSpec(memory_space=pltpu.SMEM)
ANY = pl.BlockSpec(memory_space=pl.ANY)

PANEL_ROUNDS = (
    ("n00n", ((1, 0), (2, 0), (2, 1), (1, 1))),
    ("011x", (None, (2, 0), (2, 1), (0, 1))),
    ("0nn0", ((0, 1), (1, 1), (1, 0), None)),
    ("1x00", ((0, 1), (0, 1), None, None)),
)
SHARES = (0, 2, 1, 3)
PORTIONS = (2, 2, 2, 2, 2, 2)


def dot(a, b):
    return jnp.dot(a, b, precision=lax.Precision.HIGHEST, preferred_element_type=F32)


def plain(left, upper, row_blocks, col_blocks, ancestor):
    row_on = jnp.repeat((row_blocks[0] > 0).astype(F32), left.shape[0] // row_blocks.shape[1])[:, None]
    col_on = jnp.repeat((col_blocks[0] > 0).astype(F32), upper.shape[1] // col_blocks.shape[1])[None, :]
    upper_full = lax.all_gather(upper, "row", axis=0, tiled=True)
    lower_full = lax.all_gather(left * row_on, "col", axis=1, tiled=True)
    leaf_count = lax.axis_size("leaf")
    share_cols = upper.shape[1] // leaf_count
    schur = lax.psum_scatter(dot(lower_full, upper_full) * col_on, "leaf", scatter_dimension=1, tiled=True)
    share = lax.dynamic_slice_in_dim(ancestor, lax.axis_index("leaf") * share_cols, share_cols, 1)
    updated = share - schur
    peak = lax.pmax(jnp.max(jnp.abs(updated), axis=1), ("leaf", "col"))
    return updated / (peak[:, None] + 1e-6)


def run(body, ins, outs, flops=0, limit=24):
    size = sum(4 * a.size for s, a in ins if s is VMEM) + sum(4 * o.size for o in outs)

    def whole(a):
        return pl.BlockSpec(a.shape, lambda step: (0,) * len(a.shape))

    return pl.pallas_call(
        body,
        grid=(1,),
        in_specs=[whole(a) if s is VMEM else s for s, a in ins],
        out_specs=[whole(o) for o in outs],
        out_shape=outs,
        compiler_params=pltpu.CompilerParams(vmem_limit_bytes=limit * 2**20),
        cost_estimate=pl.CostEstimate(flops=flops, bytes_accessed=size, transcendentals=0),
    )(*[a for _, a in ins])


def shape(*dims, dtype=F32):
    return jax.ShapeDtypeStruct(dims, dtype)


def split(x):
    high = x.astype(BF16)
    return high, (x - high.astype(F32)).astype(BF16)


def product(ah, al, b):
    bh, bl = split(b)
    d = functools.partial(jnp.dot, preferred_element_type=F32)
    return d(ah, bh) + (d(ah, bl) + d(al, bh))


def coordinates():
    row = lax.axis_index("row")
    return row % 2 == 1, row // 2 == 1, lax.axis_index("col") == 1


def pick(y, c, a, b, cc, d):
    return jnp.where(c, jnp.where(y, d, b), jnp.where(y, cc, a))


def copy_chunk(tiles, out, chunk):
    at, wide = chunk
    each = len(tiles) // len(SHARES)
    for k in range(len(SHARES)):
        done = 0
        for m in range(each):
            skip = (at + done) % LANES
            take = min(LANES - skip, wide - done)
            out[:, pl.ds(k * wide + done, take)] = tiles[k * each + m][:, pl.ds(skip, take)]
            done += take


def copy_message(tiles, out, chunks):
    at = 0
    for chunk in chunks:
        count = len(SHARES) * spanned(chunk)
        copy_chunk(tiles[:count], out.at[:, pl.ds(at, len(SHARES) * chunk[1])], chunk)
        tiles, at = tiles[count:], at + len(SHARES) * chunk[1]


def message_body(chunks, token, *refs):
    copy_message(refs[:-1], refs[-1], chunks)


def first_body(chunks, row_blocks, left, *refs):
    x, y, c = coordinates()
    depth = left.shape[1] // 2
    mask = jnp.where(row_blocks[0, 0] > 0, 1.0, 0.0).astype(F32)
    l0, l1 = left[:, :depth] * mask, left[:, depth:] * mask
    named = {"0": l0, "1": l1, "x": jnp.where(x, l1, l0), "n": jnp.where(x, l0, l1)}
    count = sum(len(SHARES) * spanned(c0) for c0 in chunks)
    tiles, outs = refs[:count], refs[count:]
    for out, (index, _) in zip(outs, PANEL_ROUNDS):
        out[...] = pick(y, c, *(named[k] for k in index))
    outs[4][:, :depth] = l0
    outs[4][:, depth:] = l1
    copy_message(tiles, outs[5], chunks)


def spanned(chunk):
    at, wide = chunk
    return (at + wide - 1) // LANES - at // LANES + 1


def panel_body(left, *refs):
    x, y, c = coordinates()
    height, depth = left.shape[0], left.shape[1] // 2
    r1, r2, r3, r4 = (r[...] for r in refs[:4])
    l0, l1 = left[:, :depth], left[:, depth:]
    lx = jnp.where(x, l1, l0)
    partner = pick(y, c, r1, r1, r3, r1), pick(y, c, r3, r2, r1, r2)
    own = pick(y, c, lx, r3, lx, l0), pick(y, c, r4, r4, r2, l1)
    second = jnp.logical_or(jnp.logical_and(c, x), jnp.logical_and(jnp.logical_not(c), y))
    for at in (0, 1):
        high, low = refs[4 + 2 * at:6 + 2 * at]
        for rows, pair in ((pl.ds(0, height), partner), (pl.ds(height, height), own)):
            a, b = pair[::-1] if at else pair
            high[rows], low[rows] = split(jnp.where(second, b, a))


def multiply_body(half, plan, col_blocks, ah, al, bh, bl, block, got, token, *refs):
    ranges, begin, wide, later = plan
    tiles, (send, keep), rest = refs[:-2 - bool(later)], refs[len(refs) - 2 - bool(later):][:2], refs[-1]
    own, other = block[:, pl.ds(begin, wide)], got[:, pl.ds(begin, wide)]
    for out, rows in ((send, pl.ds(0, half)), (keep, pl.ds(half, half))):
        value = product(ah[rows], al[rows], own) + product(bh[rows], bl[rows], other)
        for at, width, b in ranges:
            on = jnp.where(col_blocks[0, b] > 0, 1.0, 0.0).astype(F32)
            out[:, pl.ds(at, width)] = value[:, at:at + width] * on
    if later:
        copy_message(tiles, rest, later)


def reduce_body(jobs, *refs):
    n_in = sum(count for _, count, _ in jobs)
    ins, outs = list(refs[:n_in]), list(refs[n_in + 1:])
    leaf = lax.axis_index("leaf")
    for step, count, wide in jobs:
        mine, ins = ins[:count], ins[count:]
        send, keep, outs = outs[0], outs[1], outs[2:]
        if step == "f":
            got, *kept, share, peak = mine
            at, top = 0, None
            for piece in kept:
                lanes = pl.ds(at, piece.shape[1])
                value = share[:, lanes] - (piece[...] + got[:, lanes])
                send[:, lanes] = value
                high = jnp.max(jnp.abs(value), axis=1, keepdims=True)
                top = high if top is None else jnp.maximum(top, high)
                at += piece.shape[1]
            keep[...] = jnp.maximum(peak[...], jnp.broadcast_to(top, keep.shape))
            continue
        bit = (leaf % 2 if step == "o" else leaf // 2) == 1
        half = 2 * wide if step == "o" else wide
        total = mine[0][...] + mine[1][...]
        a, b = total[:, :half], total[:, half:]
        at = 0
        for earlier in mine[2:]:
            send[:, pl.ds(at, earlier.shape[1])] = earlier[...]
            at += earlier.shape[1]
        send[:, pl.ds(at, half)] = jnp.where(bit, a, b)
        keep[...] = jnp.where(bit, b, a)


def swap(value, axis, size, bit):
    return lax.ppermute(value, axis, [(i, i ^ bit) for i in range(size)])


def after(value, *others):
    return lax.optimization_barrier((value,) + others)[0]


STEPS = (
    "A0", "A1", "o0", "A2", "o1t0", "A3", "o2t1", "A4", "o3t2", "f1", "A5", "o4t3", "o5t4", "f3", "t5", "f4", "f5",
)
GATHERS = ((0,), (1,), (2,), (3,), (4,), (5,))
TIES = (None, None, 0, 1, 2, 3)
FIRST = 56
GROUPS = ((0, 1), (2, 3), (4,), (5,))


def chunked(left, upper, row_blocks, col_blocks, ancestor):
    rows, cols = lax.axis_size("row"), lax.axis_size("col")
    leaf_count = lax.axis_size("leaf")
    leaf, row, col = (lax.axis_index(a).astype(jnp.int32) for a in ("leaf", "row", "col"))
    depth, height = upper.shape[0], left.shape[0]
    share_cols = upper.shape[1] // leaf_count
    block_cols = upper.shape[1] // col_blocks.shape[1]
    unit = share_cols // sum(PORTIONS)
    chunks, at = [], 0
    for p in PORTIONS:
        chunks.append((at, p * unit))
        at += p * unit
    n = len(chunks)
    def move(value, flip):
        pairs = []
        for r in range(rows):
            for c in range(cols):
                hop = flip(r, c)
                if hop is not None:
                    pairs.append((cols * r + c, cols * (r ^ hop[0]) + (c ^ hop[1])))
        return lax.ppermute(value, ("row", "col"), pairs)

    def gather(value):
        return move(value, lambda r, c: (1 if c else 2, 0))

    def exchange(value):
        return move(value, lambda r, c: (2 if c else 1, 0))

    def tiles(chunk):
        at, _ = chunk
        return [
            (pl.BlockSpec((depth, LANES), functools.partial(lambda k, step: (0, k), (s * share_cols + at) // LANES + m)), upper)
            for s in SHARES for m in range(spanned(chunk))
        ]

    def tiles_of(members):
        return [spec for i in members for spec in tiles(chunks[i])]

    def widths(members):
        return 4 * sum(chunks[i][1] for i in members)

    first = run(
        functools.partial(first_body, [chunks[i] for i in GATHERS[0]]),
        [(SMEM, row_blocks), (VMEM, left)] + tiles_of(GATHERS[0]),
        [shape(height, depth)] * 4 + [shape(height, 2 * depth), shape(depth, widths(GATHERS[0]))],
        limit=FIRST,
    )
    blocks, gots = {0: first[5]}, {0: gather(first[5])}
    landed = [move(v, lambda r, c, hops=hops: hops[(r // 2) * 2 + c]) for v, (_, hops) in zip(first[:4], PANEL_ROUNDS)]
    lower = first[4]
    for g, tie in enumerate(TIES):
        if g and tie is None:
            blocks[g], = run(
                functools.partial(message_body, [chunks[i] for i in GATHERS[g]]),
                [(ANY, lower)] + tiles_of(GATHERS[g]), [shape(depth, widths(GATHERS[g]))], limit=FIRST,
            )
            gots[g] = gather(blocks[g])
    halves = run(panel_body, [(VMEM, lower)] + [(VMEM, v) for v in landed], [shape(2 * height, depth, dtype=BF16)] * 4)

    share = lax.dynamic_slice_in_dim(after(ancestor, halves[0]), leaf * share_cols, share_cols, 1)
    waiting = {}
    x_got, kept, z1, z1_kept, z2, z2_kept, upds = ({} for _ in range(7))
    peak = jnp.zeros((height, LANES), F32)
    token = a_token = lower
    for word in STEPS:
        if word[0] == "A":
            t = int(word[1:])
            at, wide = chunks[t]
            ranges = []
            for k, s in enumerate(SHARES):
                start = s * share_cols + at
                end, base = start + wide, start
                while start < end:
                    stop = min(end, (start // block_cols + 1) * block_cols)
                    ranges.append((k * wide + start - base, stop - start, start // block_cols))
                    start = stop
            g = [t in members for members in GATHERS].index(True)
            begin = widths([i for i in GATHERS[g] if i < t])
            later = [k for k, tie in enumerate(TIES) if tie == t]
            members = [chunks[i] for k in later for i in GATHERS[k]]
            res = run(
                functools.partial(multiply_body, height, (ranges, begin, 4 * wide, members)),
                [(SMEM, col_blocks)] + [(VMEM, h) for h in halves] + [(VMEM, blocks[g]), (VMEM, gots[g]), (ANY, a_token)]
                + [spec for k in later for spec in tiles_of(GATHERS[k])],
                [shape(height, 4 * wide)] * 2 + [shape(depth, widths(GATHERS[k])) for k in later],
                flops=48 * height * depth * wide,
            )
            kept[t] = a_token = res[1]
            token = res[1]
            for k in later:
                blocks[k] = res[2]
                gots[k] = gather(res[2])
            x_got[t] = exchange(res[0])
            continue
        todo = [(word[i], int(word[i + 1])) for i in range(0, len(word), 2)]
        jobs, ins, outs = [], [], []
        for step, t in todo:
            at, wide = chunks[t]
            if step == "o":
                mine, new = [x_got[t], kept[t]], [shape(height, 2 * wide)] * 2
            elif step == "t":
                group = [g for g in GROUPS if t in g][0]
                before = [waiting[i] for i in group[:-1]] if t == group[-1] else []
                mine = [z1[t], z1_kept[t]] + before
                new = [shape(height, wide + sum(b.shape[1] for b in before)), shape(height, wide)]
            else:
                group = [g for g in GROUPS if t in g][0]
                at, wide = chunks[group[0]][0], sum(chunks[i][1] for i in group)
                mine = [z2[t]] + [z2_kept[i] for i in group] + [share[:, at:at + wide], peak]
                new = [shape(height, wide), shape(height, LANES)]
            jobs.append((step, len(mine), wide))
            ins += [(VMEM, v) for v in mine]
            outs += new
        res = run(functools.partial(reduce_body, jobs), ins + [(ANY, token)], outs)
        token = res[1]
        a_token = res[1]
        tops = []
        for k, (step, t) in enumerate(todo):
            a, b = res[2 * k], res[2 * k + 1]
            if step == "o":
                z1[t], z1_kept[t] = swap(a, "leaf", leaf_count, 1), b
            elif step == "t":
                waiting[t], z2_kept[t] = a, b
                if t in [g[-1] for g in GROUPS]:
                    z2[t] = swap(a, "leaf", leaf_count, 2)
            else:
                upds[t] = a
                tops.append(b)
        if tops:
            peak = functools.reduce(jnp.maximum, tops)

    updated = jnp.concatenate([upds[g[-1]] for g in GROUPS], 1)
    top = jnp.max(peak, axis=1)
    top = jnp.maximum(top, swap(top, "col", cols, 1))
    for bit in (1, 2):
        top = jnp.maximum(top, swap(top, "leaf", leaf_count, bit))
    return updated / (top[:, None] + 1e-6)


def solution(mesh):
    leaf_count, rows, cols = (mesh.shape[a] for a in ("leaf", "row", "col"))

    def shards(left_panels, upper_panels, row_blocks, col_blocks, ancestor):
        share_cols = upper_panels.shape[2] // leaf_count
        fits = (
            rows == 4 and cols == 2 and leaf_count == 4
            and share_cols % (sum(PORTIONS) * 64) == 0
            and left_panels.shape[2] == 2 * upper_panels.shape[1]
            and row_blocks.shape[1] == 1
        )
        body = chunked if fits else plain
        return body(left_panels[0], upper_panels[0], row_blocks, col_blocks, ancestor)

    return jax.shard_map(
        shards,
        mesh=mesh,
        in_specs=(
            P("leaf", "row", "col"),
            P("leaf", "row", "col"),
            P("leaf", "row"),
            P("leaf", "col"),
            P("row", "col"),
        ),
        out_specs=P("row", ("col", "leaf")),
        check_vma=False,
    )
```

```python
import functools

import jax
import jax.numpy as jnp
from jax import lax
from jax.experimental import pallas as pl
from jax.experimental.pallas import tpu as pltpu
from jax.sharding import PartitionSpec as P

LANES = 128
F32, BF16 = jnp.float32, jnp.bfloat16
VMEM = "whole"
SMEM = pl.BlockSpec(memory_space=pltpu.SMEM)
ANY = pl.BlockSpec(memory_space=pl.ANY)

PANEL_ROUNDS = (
    ("n00n", ((1, 0), (2, 0), (2, 1), (1, 1))),
    ("011x", (None, (2, 0), (2, 1), (0, 1))),
    ("0nn0", ((0, 1), (1, 1), (1, 0), None)),
    ("1x00", ((0, 1), (0, 1), None, None)),
)
SHARES = (0, 2, 1, 3)
PORTIONS = (2, 2, 2, 2, 2, 2)


def dot(a, b):
    return jnp.dot(a, b, precision=lax.Precision.HIGHEST, preferred_element_type=F32)


def plain(left, upper, row_blocks, col_blocks, ancestor):
    row_on = jnp.repeat((row_blocks[0] > 0).astype(F32), left.shape[0] // row_blocks.shape[1])[:, None]
    col_on = jnp.repeat((col_blocks[0] > 0).astype(F32), upper.shape[1] // col_blocks.shape[1])[None, :]
    upper_full = lax.all_gather(upper, "row", axis=0, tiled=True)
    lower_full = lax.all_gather(left * row_on, "col", axis=1, tiled=True)
    leaf_count = lax.axis_size("leaf")
    share_cols = upper.shape[1] // leaf_count
    schur = lax.psum_scatter(dot(lower_full, upper_full) * col_on, "leaf", scatter_dimension=1, tiled=True)
    share = lax.dynamic_slice_in_dim(ancestor, lax.axis_index("leaf") * share_cols, share_cols, 1)
    updated = share - schur
    peak = lax.pmax(jnp.max(jnp.abs(updated), axis=1), ("leaf", "col"))
    return updated / (peak[:, None] + 1e-6)


def run(body, ins, outs, flops=0, limit=24):
    size = sum(4 * a.size for s, a in ins if s is VMEM) + sum(4 * o.size for o in outs)

    def whole(a):
        return pl.BlockSpec(a.shape, lambda step: (0,) * len(a.shape))

    return pl.pallas_call(
        body,
        grid=(1,),
        in_specs=[whole(a) if s is VMEM else s for s, a in ins],
        out_specs=[whole(o) for o in outs],
        out_shape=outs,
        compiler_params=pltpu.CompilerParams(vmem_limit_bytes=limit * 2**20),
        cost_estimate=pl.CostEstimate(flops=flops, bytes_accessed=size, transcendentals=0),
    )(*[a for _, a in ins])


def shape(*dims, dtype=F32):
    return jax.ShapeDtypeStruct(dims, dtype)


def split(x):
    high = x.astype(BF16)
    return high, (x - high.astype(F32)).astype(BF16)


def product(ah, al, b):
    bh, bl = split(b)
    d = functools.partial(jnp.dot, preferred_element_type=F32)
    return d(ah, bh) + (d(ah, bl) + d(al, bh))


def coordinates():
    row = lax.axis_index("row")
    return row % 2 == 1, row // 2 == 1, lax.axis_index("col") == 1


def pick(y, c, a, b, cc, d):
    return jnp.where(c, jnp.where(y, d, b), jnp.where(y, cc, a))


def copy_chunk(tiles, out, chunk):
    at, wide = chunk
    each = len(tiles) // len(SHARES)
    for k in range(len(SHARES)):
        done = 0
        for m in range(each):
            skip = (at + done) % LANES
            take = min(LANES - skip, wide - done)
            out[:, pl.ds(k * wide + done, take)] = tiles[k * each + m][:, pl.ds(skip, take)]
            done += take


def copy_message(tiles, out, chunks):
    at = 0
    for chunk in chunks:
        count = len(SHARES) * spanned(chunk)
        copy_chunk(tiles[:count], out.at[:, pl.ds(at, len(SHARES) * chunk[1])], chunk)
        tiles, at = tiles[count:], at + len(SHARES) * chunk[1]


def message_body(chunks, token, *refs):
    copy_message(refs[:-1], refs[-1], chunks)


def first_body(chunks, row_blocks, left, *refs):
    x, y, c = coordinates()
    depth = left.shape[1] // 2
    mask = jnp.where(row_blocks[0, 0] > 0, 1.0, 0.0).astype(F32)
    l0, l1 = left[:, :depth] * mask, left[:, depth:] * mask
    named = {"0": l0, "1": l1, "x": jnp.where(x, l1, l0), "n": jnp.where(x, l0, l1)}
    count = sum(len(SHARES) * spanned(c0) for c0 in chunks)
    tiles, outs = refs[:count], refs[count:]
    for out, (index, _) in zip(outs, PANEL_ROUNDS):
        out[...] = pick(y, c, *(named[k] for k in index))
    copy_message(tiles, outs[4], chunks)


def spanned(chunk):
    at, wide = chunk
    return (at + wide - 1) // LANES - at // LANES + 1


def panel_body(row_blocks, left, *refs):
    x, y, c = coordinates()
    height, depth = left.shape[0], left.shape[1] // 2
    r1, r2, r3, r4 = (r[...] for r in refs[:4])
    mask = jnp.where(row_blocks[0, 0] > 0, 1.0, 0.0).astype(F32)
    l0, l1 = left[:, :depth] * mask, left[:, depth:] * mask
    lx = jnp.where(x, l1, l0)
    partner = pick(y, c, r1, r1, r3, r1), pick(y, c, r3, r2, r1, r2)
    own = pick(y, c, lx, r3, lx, l0), pick(y, c, r4, r4, r2, l1)
    second = jnp.logical_or(jnp.logical_and(c, x), jnp.logical_and(jnp.logical_not(c), y))
    for at in (0, 1):
        high, low = refs[4 + 2 * at:6 + 2 * at]
        for rows, pair in ((pl.ds(0, height), partner), (pl.ds(height, height), own)):
            a, b = pair[::-1] if at else pair
            high[rows], low[rows] = split(jnp.where(second, b, a))


def multiply_body(half, plan, col_blocks, ah, al, bh, bl, block, got, token, *refs):
    ranges, begin, wide, later = plan
    tiles, (send, keep), rest = refs[:-2 - bool(later)], refs[len(refs) - 2 - bool(later):][:2], refs[-1]
    own, other = block[:, pl.ds(begin, wide)], got[:, pl.ds(begin, wide)]
    for out, rows in ((send, pl.ds(0, half)), (keep, pl.ds(half, half))):
        value = product(ah[rows], al[rows], own) + product(bh[rows], bl[rows], other)
        for at, width, b in ranges:
            on = jnp.where(col_blocks[0, b] > 0, 1.0, 0.0).astype(F32)
            out[:, pl.ds(at, width)] = value[:, at:at + width] * on
    if later:
        copy_message(tiles, rest, later)


def reduce_body(jobs, *refs):
    n_in = sum(count for _, count, _ in jobs)
    ins, outs = list(refs[:n_in]), list(refs[n_in + 1:])
    leaf = lax.axis_index("leaf")
    for step, count, wide in jobs:
        mine, ins = ins[:count], ins[count:]
        send, keep, outs = outs[0], outs[1], outs[2:]
        if step == "f":
            got, *kept, share, peak = mine
            at, top = 0, None
            for piece in kept:
                lanes = pl.ds(at, piece.shape[1])
                value = share[:, lanes] - (piece[...] + got[:, lanes])
                send[:, lanes] = value
                high = jnp.max(jnp.abs(value), axis=1, keepdims=True)
                top = high if top is None else jnp.maximum(top, high)
                at += piece.shape[1]
            keep[...] = jnp.maximum(peak[...], jnp.broadcast_to(top, keep.shape))
            continue
        bit = (leaf % 2 if step == "o" else leaf // 2) == 1
        half = 2 * wide if step == "o" else wide
        total = mine[0][...] + mine[1][...]
        a, b = total[:, :half], total[:, half:]
        at = 0
        for earlier in mine[2:]:
            send[:, pl.ds(at, earlier.shape[1])] = earlier[...]
            at += earlier.shape[1]
        send[:, pl.ds(at, half)] = jnp.where(bit, a, b)
        keep[...] = jnp.where(bit, b, a)


def swap(value, axis, size, bit):
    return lax.ppermute(value, axis, [(i, i ^ bit) for i in range(size)])


def after(value, *others):
    return lax.optimization_barrier((value,) + others)[0]


STEPS = (
    "A0", "A1", "o0", "A2", "o1t0", "A3", "o2t1", "A4", "o3t2", "f1", "A5", "o4t3", "o5t4", "f3", "t5", "f4", "f5",
)
GATHERS = ((0,), (1,), (2,), (3,), (4,), (5,))
TIES = (None, None, 0, 1, 2, 3)
FIRST = 56
GROUPS = ((0, 1), (2, 3), (4,), (5,))


def chunked(left, upper, row_blocks, col_blocks, ancestor):
    rows, cols = lax.axis_size("row"), lax.axis_size("col")
    leaf_count = lax.axis_size("leaf")
    leaf, row, col = (lax.axis_index(a).astype(jnp.int32) for a in ("leaf", "row", "col"))
    depth, height = upper.shape[0], left.shape[0]
    share_cols = upper.shape[1] // leaf_count
    block_cols = upper.shape[1] // col_blocks.shape[1]
    unit = share_cols // sum(PORTIONS)
    chunks, at = [], 0
    for p in PORTIONS:
        chunks.append((at, p * unit))
        at += p * unit
    n = len(chunks)
    def move(value, flip):
        pairs = []
        for r in range(rows):
            for c in range(cols):
                hop = flip(r, c)
                if hop is not None:
                    pairs.append((cols * r + c, cols * (r ^ hop[0]) + (c ^ hop[1])))
        return lax.ppermute(value, ("row", "col"), pairs)

    def gather(value):
        return move(value, lambda r, c: (1 if c else 2, 0))

    def exchange(value):
        return move(value, lambda r, c: (2 if c else 1, 0))

    def tiles(chunk):
        at, _ = chunk
        return [
            (pl.BlockSpec((depth, LANES), functools.partial(lambda k, step: (0, k), (s * share_cols + at) // LANES + m)), upper)
            for s in SHARES for m in range(spanned(chunk))
        ]

    def tiles_of(members):
        return [spec for i in members for spec in tiles(chunks[i])]

    def widths(members):
        return 4 * sum(chunks[i][1] for i in members)

    first = run(
        functools.partial(first_body, [chunks[i] for i in GATHERS[0]]),
        [(SMEM, row_blocks), (VMEM, left)] + tiles_of(GATHERS[0]),
        [shape(height, depth)] * 4 + [shape(depth, widths(GATHERS[0]))],
        limit=FIRST,
    )
    blocks, gots = {0: first[4]}, {0: gather(first[4])}
    landed = [move(v, lambda r, c, hops=hops: hops[(r // 2) * 2 + c]) for v, (_, hops) in zip(first[:4], PANEL_ROUNDS)]
    lower = first[0]
    for g, tie in enumerate(TIES):
        if g and tie is None:
            blocks[g], = run(
                functools.partial(message_body, [chunks[i] for i in GATHERS[g]]),
                [(ANY, lower)] + tiles_of(GATHERS[g]), [shape(depth, widths(GATHERS[g]))], limit=FIRST,
            )
            gots[g] = gather(blocks[g])
    halves = run(panel_body, [(SMEM, row_blocks), (VMEM, left)] + [(VMEM, v) for v in landed], [shape(2 * height, depth, dtype=BF16)] * 4)

    share = lax.dynamic_slice_in_dim(after(ancestor, halves[0]), leaf * share_cols, share_cols, 1)
    waiting = {}
    x_got, kept, z1, z1_kept, z2, z2_kept, upds = ({} for _ in range(7))
    peak = jnp.zeros((height, LANES), F32)
    token = a_token = lower
    for word in STEPS:
        if word[0] == "A":
            t = int(word[1:])
            at, wide = chunks[t]
            ranges = []
            for k, s in enumerate(SHARES):
                start = s * share_cols + at
                end, base = start + wide, start
                while start < end:
                    stop = min(end, (start // block_cols + 1) * block_cols)
                    ranges.append((k * wide + start - base, stop - start, start // block_cols))
                    start = stop
            g = [t in members for members in GATHERS].index(True)
            begin = widths([i for i in GATHERS[g] if i < t])
            later = [k for k, tie in enumerate(TIES) if tie == t]
            members = [chunks[i] for k in later for i in GATHERS[k]]
            res = run(
                functools.partial(multiply_body, height, (ranges, begin, 4 * wide, members)),
                [(SMEM, col_blocks)] + [(VMEM, h) for h in halves] + [(VMEM, blocks[g]), (VMEM, gots[g]), (ANY, a_token)]
                + [spec for k in later for spec in tiles_of(GATHERS[k])],
                [shape(height, 4 * wide)] * 2 + [shape(depth, widths(GATHERS[k])) for k in later],
                flops=48 * height * depth * wide,
            )
            kept[t] = a_token = res[1]
            token = res[1]
            for k in later:
                blocks[k] = res[2]
                gots[k] = gather(res[2])
            x_got[t] = exchange(res[0])
            continue
        todo = [(word[i], int(word[i + 1])) for i in range(0, len(word), 2)]
        jobs, ins, outs = [], [], []
        for step, t in todo:
            at, wide = chunks[t]
            if step == "o":
                mine, new = [x_got[t], kept[t]], [shape(height, 2 * wide)] * 2
            elif step == "t":
                group = [g for g in GROUPS if t in g][0]
                before = [waiting[i] for i in group[:-1]] if t == group[-1] else []
                mine = [z1[t], z1_kept[t]] + before
                new = [shape(height, wide + sum(b.shape[1] for b in before)), shape(height, wide)]
            else:
                group = [g for g in GROUPS if t in g][0]
                at, wide = chunks[group[0]][0], sum(chunks[i][1] for i in group)
                mine = [z2[t]] + [z2_kept[i] for i in group] + [share[:, at:at + wide], peak]
                new = [shape(height, wide), shape(height, LANES)]
            jobs.append((step, len(mine), wide))
            ins += [(VMEM, v) for v in mine]
            outs += new
        res = run(functools.partial(reduce_body, jobs), ins + [(ANY, token)], outs)
        token = res[1]
        a_token = res[1]
        tops = []
        for k, (step, t) in enumerate(todo):
            a, b = res[2 * k], res[2 * k + 1]
            if step == "o":
                z1[t], z1_kept[t] = swap(a, "leaf", leaf_count, 1), b
            elif step == "t":
                waiting[t], z2_kept[t] = a, b
                if t in [g[-1] for g in GROUPS]:
                    z2[t] = swap(a, "leaf", leaf_count, 2)
            else:
                upds[t] = a
                tops.append(b)
        if tops:
            peak = functools.reduce(jnp.maximum, tops)

    updated = jnp.concatenate([upds[g[-1]] for g in GROUPS], 1)
    top = jnp.max(peak, axis=1)
    top = jnp.maximum(top, swap(top, "col", cols, 1))
    for bit in (1, 2):
        top = jnp.maximum(top, swap(top, "leaf", leaf_count, bit))
    return updated / (top[:, None] + 1e-6)


def solution(mesh):
    leaf_count, rows, cols = (mesh.shape[a] for a in ("leaf", "row", "col"))

    def shards(left_panels, upper_panels, row_blocks, col_blocks, ancestor):
        share_cols = upper_panels.shape[2] // leaf_count
        fits = (
            rows == 4 and cols == 2 and leaf_count == 4
            and share_cols % (sum(PORTIONS) * 64) == 0
            and left_panels.shape[2] == 2 * upper_panels.shape[1]
            and row_blocks.shape[1] == 1
        )
        body = chunked if fits else plain
        return body(left_panels[0], upper_panels[0], row_blocks, col_blocks, ancestor)

    return jax.shard_map(
        shards,
        mesh=mesh,
        in_specs=(
            P("leaf", "row", "col"),
            P("leaf", "row", "col"),
            P("leaf", "row"),
            P("leaf", "col"),
            P("row", "col"),
        ),
        out_specs=P("row", ("col", "leaf")),
        check_vma=False,
    )
```
